256 devices in a mesh: group: 32 (over z, y_lo, core), fsdp: 8 (over y_hi, x).
Axes of the slice: x: 4, y: 4 (y_hi: 2, y_lo: 2; y = y_hi * 2 + y_lo), z: 8, core: 2. Of those that a mesh axis runs over, the one named last changes fastest.
Arguments:
- inputs: bfloat16 [32, 4, 256, 4096], P('group', None, 'fsdp'), may hold values from -6 to 6
- cotangent: bfloat16 [32, 4, 256, 4096], P('group', None, 'fsdp'), may hold values from -6 to 6
- value_weight: bfloat16 [32, 4096, 2048], P('group', 'fsdp'), may hold values from -6 to 6
- output_weight: bfloat16 [32, 2048, 4096], P('group', 'fsdp'), may hold values from -6 to 6
- push_weight: float32 [32], P('group'), may hold values from 0.5 to 2
- position_bias: float32 [32, 32, 32], replicated, may hold values from -8 to 300
- step_index: int32 [1], replicated, may hold values from 0 to 999
Outputs:
- value_out: bfloat16 [32, 4096, 2048], P('group', 'fsdp')
- output_out: bfloat16 [32, 2048, 4096], P('group', 'fsdp')
- mass_out: float32 [32], P('group')
The draws below stay inside these ranges and needn't reach their ends.
All inputs are finite; a program needn't handle non-finite values.
Results may differ from the reference program's by a relative error of at most 0.015.
Values may be sent and summed in bfloat16 or wider, within the bound.
A program may use at most 192 MiB of HBM per device.

```python
import math
import jax
import jax.numpy as jnp
from jax import lax

D = 4096
HDIM = 64
HEADS = 32
SEQ = 32
STEPS = 4
GROUPS = 32
BATCH = 256
N_FSDP = 8


def draw_position_bias(key, part):
    key = jax.random.fold_in(key, 7)
    keys = jax.random.split(key, 1)
    logits = jnp.clip(jax.random.normal(keys[0], (HEADS, SEQ, SEQ), jnp.float32) * 2.0, -8.0, 8.0)
    return logits.astype(jnp.float32)


def block_levels(rng, extent, cuts, least, largest):
    factor_of = 1.0
    for position, parts in cuts:
        heights = jax.random.uniform(jax.random.fold_in(jax.random.fold_in(rng, 6), position), (parts,), jnp.float32, least / len(cuts), largest / len(cuts))
        factor_of = factor_of * jnp.repeat(jnp.exp(heights), extent[position] // parts).reshape((-1,) + (1,) * (len(extent) - 1 - position))
    return factor_of


def scatter_about(stream_key, dims, width, limit, cuts=(), held_as=jnp.bfloat16):
    result = width * jax.random.normal(stream_key, dims, jnp.float32)
    if cuts:
        result = result * block_levels(stream_key, dims, cuts, -0.22, 0.18)
    return jnp.clip(result, -limit, limit).astype(held_as)


def setup_inputs(seed: int = 0) -> dict:
    seeds = jax.random.split(jax.random.key(seed), 8)
    inputs = scatter_about(seeds[0], (GROUPS, STEPS, BATCH, D), 1.0, 6.0, ((0, 32), (2, 8)))
    cotangent = scatter_about(seeds[1], (GROUPS, STEPS, BATCH, D), 1.0, 6.0, ((0, 32), (2, 8)))
    value_weight = scatter_about(seeds[2], (GROUPS, D, HEADS * HDIM), 1.0, 6.0, ((0, 32), (1, 8)))
    output_weight = scatter_about(seeds[3], (GROUPS, HEADS * HDIM, D), 1.0, 6.0, ((0, 32), (1, 8)))
    push_weight = jnp.clip(jnp.exp(math.log(2.0) - 1.3862944 * jax.random.uniform(seeds[4], (GROUPS,), jnp.float32) ** block_levels(seeds[4], (GROUPS,), ((0, 32),), -0.2, 0.2)), 0.5, 2.0)
    position_bias = draw_position_bias(jax.random.fold_in(seeds[7], 71), 0)
    step_index = jax.random.randint(seeds[6], (1,), 0, 1000).astype(jnp.int32)
    return {"inputs": inputs, "cotangent": cotangent, "value_weight": value_weight, "output_weight": output_weight, "push_weight": push_weight, "position_bias": position_bias, "step_index": step_index}


learn_rate = 0.5

def group_step(value_num, output_num, push_mass, tokens, cotan_step, attention):
    scale_in = 1.0 / math.sqrt(D)
    scale_mid = 1.0 / math.sqrt(HEADS * HDIM)
    eff_value = (value_num / push_mass).astype(jnp.bfloat16)
    eff_output = (output_num / push_mass).astype(jnp.bfloat16)
    shard_width = D // N_FSDP
    summed = jnp.zeros((BATCH, HEADS * HDIM), jnp.float32)
    for block in range(N_FSDP):
        partial_value = jnp.dot(tokens[:, block * shard_width:(block + 1) * shard_width], eff_value[block * shard_width:(block + 1) * shard_width], preferred_element_type=jnp.float32) * scale_in
        summed = summed + partial_value.astype(jnp.bfloat16).astype(jnp.float32)
    values = summed.astype(jnp.bfloat16).reshape(N_FSDP, SEQ, HEADS, HDIM)
    weights = attention.astype(jnp.float32)
    mixed_rows = jnp.einsum('hqk,nkhe->nqhe', weights, values.astype(jnp.float32))
    mixed_rows = mixed_rows.astype(jnp.bfloat16).reshape(BATCH, HEADS * HDIM)
    dmixed = (jnp.dot(cotan_step, eff_output.T, preferred_element_type=jnp.float32) * scale_mid).astype(jnp.bfloat16)
    dvalues = jnp.einsum('hqk,nqhe->nkhe', weights, dmixed.reshape(N_FSDP, SEQ, HEADS, HDIM).astype(jnp.float32))
    dvalues = dvalues.astype(jnp.bfloat16).reshape(BATCH, HEADS * HDIM)
    grad_value = jnp.dot(tokens.T, dvalues, preferred_element_type=jnp.float32) * scale_in
    grad_output = jnp.dot(mixed_rows.T, cotan_step, preferred_element_type=jnp.float32) * scale_mid
    return ((value_num - learn_rate * grad_value) * 0.5, (output_num - learn_rate * grad_output) * 0.5)

def reference(inputs, cotangent, value_weight, output_weight, push_weight, position_bias, step_index):
    attention = jax.nn.softmax(position_bias, axis=-1).astype(jnp.bfloat16)
    value_num = value_weight.astype(jnp.float32)
    output_num = output_weight.astype(jnp.float32)
    push_mass = push_weight
    pend_value = jnp.zeros(value_weight.shape, jnp.bfloat16)
    pend_output = jnp.zeros(output_weight.shape, jnp.bfloat16)
    pend_mass = jnp.zeros(push_weight.shape, jnp.bfloat16)
    for window_step in range(STEPS):

        def single(packed):
            return group_step(packed[0], packed[1], packed[2], packed[3], packed[4], attention)
        half_value, half_output = lax.map(single, (value_num, output_num, push_mass, inputs[:, window_step], cotangent[:, window_step]))
        half_mass = push_mass * 0.5
        distance = jnp.left_shift(jnp.int32(1), ((step_index[0] + window_step) % 4).astype(jnp.int32))
        value_num = half_value + pend_value.astype(jnp.float32)
        output_num = half_output + pend_output.astype(jnp.float32)
        push_mass = half_mass + pend_mass.astype(jnp.float32)
        pend_value = jnp.roll(half_value.astype(jnp.bfloat16), distance, axis=0)
        pend_output = jnp.roll(half_output.astype(jnp.bfloat16), distance, axis=0)
        pend_mass = jnp.roll(half_mass.astype(jnp.bfloat16), distance, axis=0)
    value_num = value_num + pend_value.astype(jnp.float32)
    output_num = output_num + pend_output.astype(jnp.float32)
    push_mass = push_mass + pend_mass.astype(jnp.float32)
    value_out = (value_num / push_mass[:, None, None]).astype(jnp.bfloat16)
    output_out = (output_num / push_mass[:, None, None]).astype(jnp.bfloat16)
    return (value_out, output_out, push_mass)
```

```python
import functools
import math

import jax
import jax.numpy as jnp
from jax import lax
from jax.sharding import PartitionSpec as P

learn_rate = 0.5
DISTANCES = (1, 2, 4, 8)


def shifted(block, axis, distance):
    count = lax.axis_size(axis)
    route = [((i - distance) % count, i) for i in range(count)]
    return lax.ppermute(block, axis, route)


def contract_rows(left, right):
    return lax.dot_general(
        left, right, (((0,), (0,)), ((), ())), preferred_element_type=jnp.float32
    )


def run_window(first, columns, cot_all, attention, value_num, output_num, push_mass):
    window_steps, batch, _ = columns.shape
    heads, positions, _ = attention.shape
    inner_own = output_num.shape[0]
    head_size = inner_own // heads
    model_width = cot_all.shape[2]
    inner_width = value_num.shape[1]
    sequences = batch // positions
    scale_in = 1.0 / math.sqrt(model_width)
    scale_mid = 1.0 / math.sqrt(inner_width)
    arrived = None
    for step in range(window_steps):
        distance = DISTANCES[(first + step) % 4]
        eff_value = (value_num / push_mass[0]).astype(jnp.bfloat16)
        eff_output = (output_num / push_mass[0]).astype(jnp.bfloat16)
        cols = columns[step]
        cot = cot_all[step]
        dmixed = (
            lax.dot_general(
                cot, eff_output, (((1,), (1,)), ((), ())), preferred_element_type=jnp.float32
            )
            * scale_mid
        ).astype(jnp.bfloat16)
        dvalues = jnp.einsum(
            "hqk,nqhe->nkhe",
            attention,
            dmixed.reshape(sequences, positions, heads, head_size),
            preferred_element_type=jnp.float32,
        )
        dvalues = dvalues.astype(jnp.bfloat16).reshape(batch, inner_own)
        partial_value = jnp.dot(cols, eff_value, preferred_element_type=jnp.float32) * scale_in
        dvalues_all = lax.all_gather(dvalues, "fsdp", axis=1, tiled=True)
        values = lax.psum_scatter(
            partial_value.astype(jnp.bfloat16), "fsdp", scatter_dimension=1, tiled=True
        )
        mixed = jnp.einsum(
            "hqk,nkhe->nqhe",
            attention,
            values.reshape(sequences, positions, heads, head_size),
            preferred_element_type=jnp.float32,
        )
        mixed = mixed.astype(jnp.bfloat16).reshape(batch, inner_own)
        grad_value = contract_rows(cols, dvalues_all) * scale_in
        grad_output = contract_rows(mixed, cot) * scale_mid
        half_value = (value_num - learn_rate * grad_value) * 0.5
        half_output = (output_num - learn_rate * grad_output) * 0.5
        half_mass = push_mass * 0.5
        message = (
            half_value.astype(jnp.bfloat16),
            half_output.astype(jnp.bfloat16),
            half_mass.astype(jnp.bfloat16),
        )
        value_num, output_num, push_mass = half_value, half_output, half_mass
        if arrived is not None:
            value_num = value_num + arrived[0].astype(jnp.float32)
            output_num = output_num + arrived[1].astype(jnp.float32)
            push_mass = push_mass + arrived[2].astype(jnp.float32)
        arrived = jax.tree.map(lambda part: shifted(part, "group", distance), message)
    value_num = value_num + arrived[0].astype(jnp.float32)
    output_num = output_num + arrived[1].astype(jnp.float32)
    push_mass = push_mass + arrived[2].astype(jnp.float32)
    value_out = (value_num / push_mass[0]).astype(jnp.bfloat16)[None]
    output_out = (output_num / push_mass[0]).astype(jnp.bfloat16)[None]
    return (value_out, output_out, push_mass)


def on_device(
    inputs, cotangent, value_weight, output_weight, push_weight, position_bias, step_index
):
    head_count = position_bias.shape[0]
    own_heads = head_count // lax.axis_size("fsdp")
    bias = lax.dynamic_slice_in_dim(
        position_bias, lax.axis_index("fsdp") * own_heads, own_heads, axis=0
    )
    attention = jax.nn.softmax(bias, axis=-1).astype(jnp.bfloat16)
    value_num = value_weight[0].astype(jnp.float32)
    output_num = output_weight[0].astype(jnp.float32)
    columns = lax.all_to_all(inputs[0], "fsdp", split_axis=2, concat_axis=1, tiled=True)
    cot_all = lax.all_gather(cotangent[0], "fsdp", axis=1, tiled=True)
    branches = [functools.partial(run_window, first) for first in range(4)]
    return lax.switch(
        step_index[0] % 4,
        branches,
        columns,
        cot_all,
        attention,
        value_num,
        output_num,
        push_weight,
    )


def solution(mesh):
    placed = (
        P("group", None, "fsdp", None),
        P("group", None, "fsdp", None),
        P("group", "fsdp", None),
        P("group", "fsdp", None),
        P("group"),
        P(),
        P(),
    )
    return jax.shard_map(
        on_device,
        mesh=mesh,
        in_specs=placed,
        out_specs=(P("group", "fsdp", None), P("group", "fsdp", None), P("group")),
        check_vma=False,
    )
```

```python
import functools
import math

import jax
import jax.numpy as jnp
from jax import lax
from jax.experimental import pallas as pl
from jax.experimental.pallas import tpu as pltpu
from jax.sharding import PartitionSpec as P

DISTANCES = (1, 2, 4, 8)
MESH = pl.DeviceIdType.MESH
F32 = jnp.float32
BF16 = jnp.bfloat16


def window_kernel(
    first,
    sizes,
    inputs,
    cotangent,
    value_in,
    output_in,
    mass_in,
    bias,
    value_out,
    output_out,
    mass_out,
    x_cols,
    x_turned,
    cot_all,
    value_w,
    output_w,
    value_msg,
    output_msg,
    mass_msg,
    value_got,
    output_got,
    mass_got,
    part,
    part_got,
    dvalues_all,
    mix,
    mix_turned,
    mixed_turned,
    total,
    inverse,
    load_sem,
    own_sem,
    x_send,
    x_recv,
    cot_send,
    cot_recv,
    part_send,
    part_recv,
    dv_send,
    dv_recv,
    value_send,
    value_recv,
    output_send,
    output_recv,
    mass_send,
    mass_recv,
):
    groups, peers, steps, positions, heads, head_size = sizes
    batch = peers * positions
    v_cols = value_w.shape[2]
    o_cols = output_w.shape[2]
    x_width = x_cols.shape[3]
    scale_in = 1.0 / math.sqrt(x_width * peers)
    scale_mid = 1.0 / math.sqrt(v_cols * peers)
    g = lax.axis_index("group")
    f = lax.axis_index("fsdp")

    def peer(k):
        return lax.rem(f + k, peers)

    def ahead(distance):
        return lax.rem(g + distance, groups)

    def behind(distance):
        return lax.rem(g + groups - distance, groups)

    def remote(src, dst, send, recv, device):
        return pltpu.make_async_remote_copy(
            src_ref=src,
            dst_ref=dst,
            send_sem=send,
            recv_sem=recv,
            device_id=device,
            device_id_type=MESH,
        )

    def loads():
        for c in range(peers):
            yield pltpu.make_async_copy(
                value_in.at[0, :, pl.ds(c * v_cols, v_cols)], value_msg.at[1, c], load_sem.at[0, c]
            )
            yield pltpu.make_async_copy(
                output_in.at[0, :, pl.ds(c * o_cols, o_cols)],
                output_msg.at[1, c],
                load_sem.at[1, c],
            )

    def columns_of(p):
        return pl.ds(pl.multiple_of(p * x_width, x_width), x_width)

    own_x = pltpu.make_async_copy(
        inputs.at[0, :, :, columns_of(f)], x_cols.at[:, f], own_sem.at[0]
    )
    own_cot = pltpu.make_async_copy(cotangent.at[0], cot_all.at[:, f], own_sem.at[1])

    def x_copy(late, k):
        when = pl.ds(1, steps - 1) if late else pl.ds(0, 1)
        return remote(
            inputs.at[0, when, :, columns_of(peer(k))],
            x_cols.at[when, f],
            x_send.at[late, k],
            x_recv.at[late, k],
            (g, peer(k)),
        )

    def cot_copy(t, k):
        return remote(
            cotangent.at[0, t],
            cot_all.at[t, f],
            cot_send.at[t, k],
            cot_recv.at[t, k],
            (g, peer(k)),
        )

    def part_copy(t, k):
        return remote(
            part.at[k],
            part_got.at[t, k],
            part_send.at[t, k],
            part_recv.at[t, k],
            (g, peer(k)),
        )

    def dv_copy(t, k):
        return remote(
            dvalues_all.at[t, f],
            dvalues_all.at[t, f],
            dv_send.at[t, k],
            dv_recv.at[t, k],
            (g, peer(k)),
        )

    def target(t):
        return (ahead(DISTANCES[(first + t) % 4]), f)

    def value_copy(t, c):
        return remote(
            value_msg.at[t % 2, c],
            value_got.at[t, c],
            value_send.at[t, c],
            value_recv.at[t, c],
            target(t),
        )

    def output_copy(t, c):
        return remote(
            output_msg.at[t % 2, c],
            output_got.at[t, c],
            output_send.at[t, c],
            output_recv.at[t, c],
            target(t),
        )

    def mass_copy(t):
        return remote(
            mass_msg.at[t], mass_got.at[t], mass_send.at[t], mass_recv.at[t], target(t)
        )

    def each(body, start=0, stop=peers):
        def run(i, carry):
            body(i)
            return carry

        lax.fori_loop(start, stop, run, 0)

    for copy in loads():
        copy.start()
    own_x.start()
    own_cot.start()

    barrier = pltpu.get_barrier_semaphore()
    for k in range(1, peers):
        pl.semaphore_signal(barrier, inc=1, device_id=(g, peer(k)), device_id_type=MESH)
    for distance in DISTANCES:
        pl.semaphore_signal(barrier, inc=1, device_id=(behind(distance), f), device_id_type=MESH)
    pl.semaphore_wait(barrier, peers - 1 + len(DISTANCES))

    each(lambda k: x_copy(0, k).start(), 1)
    each(lambda k: cot_copy(0, k).start(), 1)
    each(lambda k: x_copy(1, k).start(), 1)

    for copy in loads():
        copy.wait()

    def widen(c):
        value_w[c] = value_msg[1, c].astype(F32)
        output_w[c] = output_msg[1, c].astype(F32)

    each(widen)

    spread = (
        lax.rem(lax.broadcasted_iota(jnp.int32, (batch, positions), 0), positions)
        == lax.broadcasted_iota(jnp.int32, (batch, positions), 1)
    ).astype(BF16)
    same = (
        lax.broadcasted_iota(jnp.int32, (batch, batch), 0) // positions
        == lax.broadcasted_iota(jnp.int32, (batch, batch), 1) // positions
    )
    for h in range(heads):
        logits = bias[f * heads + h]
        weights = jnp.exp(logits - jnp.max(logits, axis=-1, keepdims=True))
        weights = (weights / jnp.sum(weights, axis=-1, keepdims=True)).astype(BF16)
        for held, dims in ((mix, ((1,), (0,))), (mix_turned, ((1,), (1,)))):
            tall = lax.dot_general(spread, weights, (dims, ((), ())), preferred_element_type=F32)
            wide = lax.dot_general(
                tall.astype(BF16), spread, (((1,), (1,)), ((), ())), preferred_element_type=F32
            )
            held[h] = jnp.where(same, wide, 0.0).astype(BF16)

    head_of = lax.broadcasted_iota(jnp.int32, (batch, v_cols), 1) // head_size

    def by_heads(weights, block):
        result = jnp.zeros((batch, v_cols), F32)
        for h in range(heads):
            product = jnp.dot(weights[h], block, preferred_element_type=F32)
            result = jnp.where(head_of == h, product, result)
        return result.astype(BF16)

    mass = mass_in[...]
    own_x.wait()
    own_cot.wait()
    each(lambda k: x_copy(0, k).wait_recv(), 1)

    for t in range(steps):
        slot = t % 2
        inverse[...] = 1.0 / mass

        if t == 1:
            each(lambda k: x_copy(1, k).wait_recv(), 1)
        x_turned[...] = x_cols[t].reshape(batch, x_width).T

        def values_of(k, t=t):
            c = peer(k)
            if t >= 2:
                value_copy(t - 2, c).wait_recv()
                value_w[c] = value_w[c] + value_got[t - 2, c].astype(F32)
            effective = (value_w[c] * inverse[0:1, 0:v_cols]).astype(BF16)
            product = jnp.dot(
                x_cols[t].reshape(batch, x_width), effective, preferred_element_type=F32
            )
            return (product * scale_in).astype(BF16)

        def send_part(k, t=t, values_of=values_of):
            part[k] = values_of(k)
            part_copy(t, k).start()

        def forward(t=t, values_of=values_of, send_part=send_part):
            each(send_part, 1)
            part_got[t, 0] = values_of(0)

        def add_dmixed(c, t=t):
            if t >= 2:
                output_copy(t - 2, c).wait_recv()
                output_w[c] = output_w[c] + output_got[t - 2, c].astype(F32)
            effective = (output_w[c] * inverse[0:1, 0:o_cols]).astype(BF16)
            cot = cot_all[t, :, :, pl.ds(pl.multiple_of(c * o_cols, o_cols), o_cols)]
            total[...] += lax.dot_general(
                cot.reshape(batch, o_cols),
                effective,
                (((1,), (1,)), ((), ())),
                preferred_element_type=F32,
            )

        def backward(t=t, add_dmixed=add_dmixed):
            each(lambda k: cot_copy(t, k).wait_recv(), 1)
            total[...] = jnp.zeros_like(total)
            each(add_dmixed)
            dmixed = (total[...] * scale_mid).astype(BF16)
            dvalues_all[t, f] = by_heads(mix_turned, dmixed)
            each(lambda k: dv_copy(t, k).start(), 1)

        def update_output(c, t=t, slot=slot):
            cot = cot_all[t, :, :, pl.ds(pl.multiple_of(c * o_cols, o_cols), o_cols)]
            grad = jnp.dot(
                mixed_turned[...], cot.reshape(batch, o_cols), preferred_element_type=F32
            )
            half = 0.5 * output_w[c] - (0.25 * scale_mid) * grad
            output_w[c] = half
            if t >= 2:
                output_copy(t - 2, c).wait_send()
            output_msg[slot, c] = half.astype(BF16)
            output_copy(t, c).start()

        def outputs(t=t, update_output=update_output):
            each(lambda k: part_copy(t, k).wait(), 1)
            summed = part_got[t, 0].astype(F32)
            for k in range(1, peers):
                summed = summed + part_got[t, k].astype(F32)
            mixed_turned[...] = by_heads(mix, summed.astype(BF16)).T
            each(update_output)

        def update_value(j, t=t, slot=slot):
            c = peer(j)
            grad = jnp.dot(x_turned[...], dvalues_all[t, c], preferred_element_type=F32)
            half = 0.5 * value_w[c] - (0.25 * scale_in) * grad
            value_w[c] = half
            if t >= 2:
                value_copy(t - 2, c).wait_send()
            value_msg[slot, c] = half.astype(BF16)
            value_copy(t, c).start()

        def update_other(j, t=t, update_value=update_value):
            dv_copy(t, peers - j).wait_recv()
            update_value(j)

        def values(t=t, update_value=update_value, update_other=update_other):
            each(update_other, 1)
            update_value(0)

        half_mass = mass * 0.5
        if t < 2:
            forward()
            backward()
        else:
            backward()
            forward()
        if t + 1 < steps:
            each(lambda k: cot_copy(t + 1, k).start(), 1)
        if t < 2:
            outputs()
            values()
        else:
            values()
            outputs()
        mass_msg[t] = half_mass.astype(BF16)
        mass_copy(t).start()
        mass = half_mass
        if t >= 1:
            mass_copy(t - 1).wait_recv()
            mass = mass + mass_got[t - 1].astype(F32)

    last = steps - 1
    mass_copy(last).wait_recv()
    mass = mass + mass_got[last].astype(F32)
    mass_out[...] = mass
    inverse[...] = 1.0 / mass

    def value_store(c):
        return pltpu.make_async_copy(
            value_msg.at[0, c],
            value_out.at[0, :, pl.ds(pl.multiple_of(c * v_cols, v_cols), v_cols)],
            load_sem.at[0, c],
        )

    def output_store(c):
        return pltpu.make_async_copy(
            output_msg.at[0, c],
            output_out.at[0, :, pl.ds(pl.multiple_of(c * o_cols, o_cols), o_cols)],
            load_sem.at[1, c],
        )

    def finish_value(j):
        c = peer(j)
        value_copy(last - 1, c).wait()
        value_copy(last, c).wait_recv()
        result = (
            value_w[c] + value_got[last - 1, c].astype(F32) + value_got[last, c].astype(F32)
        )
        value_msg[0, c] = (result * inverse[0:1, 0:v_cols]).astype(BF16)
        value_store(c).start()

    def finish_output(c):
        output_copy(last - 1, c).wait()
        output_copy(last, c).wait_recv()
        result = (
            output_w[c] + output_got[last - 1, c].astype(F32) + output_got[last, c].astype(F32)
        )
        output_msg[0, c] = (result * inverse[0:1, 0:o_cols]).astype(BF16)
        output_store(c).start()

    each(finish_value, 1)
    finish_value(0)
    each(finish_output)

    def settle(k):
        x_copy(0, k).wait_send()
        x_copy(1, k).wait_send()
        for t in range(steps):
            cot_copy(t, k).wait_send()
            dv_copy(t, k).wait_send()

    each(settle, 1)

    def settle_chunk(c):
        value_copy(last, c).wait_send()
        output_copy(last, c).wait_send()
        value_store(c).wait()
        output_store(c).wait()

    each(settle_chunk)
    for t in range(steps):
        mass_copy(t).wait_send()


def run_window(first, inputs, cotangent, value_weight, output_weight, mass, bias):
    groups = lax.axis_size("group")
    peers = lax.axis_size("fsdp")
    _, steps, positions, width = inputs.shape
    rows, inner = value_weight.shape[1:]
    own_inner = output_weight.shape[1]
    heads = bias.shape[0] // peers
    head_size = own_inner // heads
    batch = positions * peers
    o_cols = width // peers
    lanes = mass.shape[1]
    dma = pltpu.SemaphoreType.DMA
    hbm = pl.BlockSpec(memory_space=pl.ANY)
    vmem = pl.BlockSpec(memory_space=pltpu.VMEM)
    sizes = (groups, peers, steps, positions, heads, head_size)
    return pl.pallas_call(
        functools.partial(window_kernel, first, sizes),
        out_shape=(
            jax.ShapeDtypeStruct(value_weight.shape, BF16),
            jax.ShapeDtypeStruct(output_weight.shape, BF16),
            jax.ShapeDtypeStruct(mass.shape, F32),
        ),
        in_specs=[hbm, hbm, hbm, hbm, vmem, vmem],
        out_specs=(hbm, hbm, vmem),
        scratch_shapes=[
            pltpu.VMEM((steps, peers, positions, rows), BF16),
            pltpu.VMEM((rows, batch), BF16),
            pltpu.VMEM((steps, peers, positions, width), BF16),
            pltpu.VMEM((peers, rows, own_inner), F32),
            pltpu.VMEM((peers, own_inner, o_cols), F32),
            pltpu.VMEM((2, peers, rows, own_inner), BF16),
            pltpu.VMEM((2, peers, own_inner, o_cols), BF16),
            pltpu.VMEM((steps, *mass.shape), BF16),
            pltpu.VMEM((steps, peers, rows, own_inner), BF16),
            pltpu.VMEM((steps, peers, own_inner, o_cols), BF16),
            pltpu.VMEM((steps, *mass.shape), BF16),
            pltpu.VMEM((peers, batch, own_inner), BF16),
            pltpu.VMEM((steps, peers, batch, own_inner), BF16),
            pltpu.VMEM((steps, peers, batch, own_inner), BF16),
            pltpu.VMEM((heads, batch, batch), BF16),
            pltpu.VMEM((heads, batch, batch), BF16),
            pltpu.VMEM((own_inner, batch), BF16),
            pltpu.VMEM((batch, own_inner), F32),
            pltpu.VMEM(mass.shape, F32),
            dma((2, peers)),
            dma((2,)),
            dma((2, peers)),
            dma((2, peers)),
            dma((steps, peers)),
            dma((steps, peers)),
            dma((steps, peers)),
            dma((steps, peers)),
            dma((steps, peers)),
            dma((steps, peers)),
            dma((steps, peers)),
            dma((steps, peers)),
            dma((steps, peers)),
            dma((steps, peers)),
            dma((steps,)),
            dma((steps,)),
        ],
        compiler_params=pltpu.CompilerParams(
            collective_id=first, has_side_effects=True, vmem_limit_bytes=63 << 20
        ),
        name="window",
    )(inputs, cotangent, value_weight, output_weight, mass, bias)


def on_device(
    inputs, cotangent, value_weight, output_weight, push_weight, position_bias, step_index
):
    mass = jnp.broadcast_to(push_weight[:, None], (16, 512))
    value_out, output_out, mass = lax.switch(
        step_index[0] % 4,
        [functools.partial(run_window, first) for first in range(4)],
        inputs,
        cotangent,
        value_weight,
        output_weight,
        mass,
        position_bias,
    )
    return (value_out, output_out, mass[0, :1])


def solution(mesh):
    placed = (
        P("group", None, "fsdp", None),
        P("group", None, "fsdp", None),
        P("group", "fsdp", None),
        P("group", "fsdp", None),
        P("group"),
        P(),
        P(),
    )
    return jax.shard_map(
        on_device,
        mesh=mesh,
        in_specs=placed,
        out_specs=(P("group", "fsdp", None), P("group", "fsdp", None), P("group")),
        check_vma=False,
    )
```

```python
import functools
import math

import jax
import jax.numpy as jnp
from jax import lax
from jax.experimental import pallas as pl
from jax.experimental.pallas import tpu as pltpu
from jax.sharding import PartitionSpec as P

DISTANCES = (1, 2, 4, 8)
RELAY = 12
SIDE = 8
PACE = ((4, 6), (2, 3), (16, 16), (16, 16))
DETOUR = ((4, 4), (4, 4), (4, 4), (4, 4))
MESH = pl.DeviceIdType.MESH
F32 = jnp.float32
BF16 = jnp.bfloat16


def window_kernel(
    first,
    sizes,
    inputs,
    cotangent,
    value_in,
    output_in,
    mass_in,
    bias,
    value_out,
    output_out,
    mass_out,
    x_cols,
    x_turned,
    cot_all,
    value_w,
    output_w,
    value_msg,
    output_msg,
    mass_msg,
    value_got,
    output_got,
    mass_got,
    part,
    part_got,
    across,
    across_got,
    relay,
    side_one,
    side_two,
    dvalues_all,
    mix,
    mix_turned,
    mixed_turned,
    total,
    inverse,
    load_sem,
    own_sem,
    x_send,
    x_recv,
    cot_send,
    cot_recv,
    part_send,
    part_recv,
    dv_send,
    dv_recv,
    value_send,
    value_recv,
    output_send,
    output_recv,
    mass_send,
    mass_recv,
    across_send,
    across_recv,
    relay_send,
    relay_recv,
    side_send,
    side_recv,
):
    groups, peers, steps, positions, heads, head_size = sizes
    batch = peers * positions
    v_cols = value_w.shape[2]
    o_cols = output_w.shape[2]
    x_width = x_cols.shape[3]
    scale_in = 1.0 / math.sqrt(x_width * peers)
    scale_mid = 1.0 / math.sqrt(v_cols * peers)
    g = lax.axis_index("group")
    f = lax.axis_index("fsdp")
    row = peers // 2
    y_half = f // row
    x_place = lax.rem(f, row)
    slow_step = (3 - first) % steps
    detour = DETOUR[first][0] + (DETOUR[first][1] - DETOUR[first][0]) * lax.rem(g // 2, 2)
    values_lead = slow_step >= 2

    def peer(k):
        return lax.rem(f + k, peers)

    def beside(j, s=0):
        return lax.rem(y_half + s, 2) * row + lax.rem(x_place + j, row)

    def chunk_at(p):
        return beside(lax.rem(p // 2 + 1, row), lax.rem(p, 2))

    def ahead(distance):
        return lax.rem(g + distance, groups)

    def behind(distance):
        return lax.rem(g + groups - distance, groups)

    def remote(src, dst, send, recv, device):
        return pltpu.make_async_remote_copy(
            src_ref=src,
            dst_ref=dst,
            send_sem=send,
            recv_sem=recv,
            device_id=device,
            device_id_type=MESH,
        )

    def loads():
        for c in range(peers):
            yield pltpu.make_async_copy(
                value_in.at[0, :, pl.ds(c * v_cols, v_cols)], value_msg.at[1, c], load_sem.at[0, c]
            )
            yield pltpu.make_async_copy(
                output_in.at[0, :, pl.ds(c * o_cols, o_cols)],
                output_msg.at[1, c],
                load_sem.at[1, c],
            )

    def columns_of(p):
        return pl.ds(pl.multiple_of(p * x_width, x_width), x_width)

    own_x = pltpu.make_async_copy(
        inputs.at[0, :, :, columns_of(f)], x_cols.at[:, f], own_sem.at[0]
    )
    own_cot = pltpu.make_async_copy(cotangent.at[0], cot_all.at[:, f], own_sem.at[1])

    def x_copy(late, k):
        when = pl.ds(1, steps - 1) if late else pl.ds(0, 1)
        return remote(
            inputs.at[0, when, :, columns_of(peer(k))],
            x_cols.at[when, f],
            x_send.at[late, k],
            x_recv.at[late, k],
            (g, peer(k)),
        )

    def cot_copy(t, k):
        block = beside(0, k // row)
        to = beside(lax.rem(k, row)) if not isinstance(k, int) else beside(0, 1)
        return remote(
            cot_all.at[t, block],
            cot_all.at[t, block],
            cot_send.at[t, k],
            cot_recv.at[t, k],
            (g, to),
        )

    def cot_first(t, k):
        to = beside(k) if not isinstance(k, int) else beside(0, 1)
        return remote(
            cotangent.at[0, t], cot_all.at[t, f], cot_send.at[t, k], cot_recv.at[t, k], (g, to)
        )

    def cot_lead(t):
        cot_first(t, 0).start()
        each(lambda j: cot_first(t, j).start(), 1, row)

    def cot_pass(t):
        cot_copy(t, 0).wait_recv()
        each(lambda j: cot_copy(t, row + j).start(), 1, row)

    def dv_copy(t, k):
        block = beside(0, k // row)
        to = beside(lax.rem(k, row)) if not isinstance(k, int) else beside(0, 1)
        return remote(
            dvalues_all.at[t, block],
            dvalues_all.at[t, block],
            dv_send.at[t, k],
            dv_recv.at[t, k],
            (g, to),
        )

    def part_copy(t, j):
        return remote(
            part.at[j],
            part_got.at[t, j],
            part_send.at[t, j],
            part_recv.at[t, j],
            (g, beside(j)),
        )

    def across_copy(t):
        return remote(
            across, across_got.at[t], across_send.at[t], across_recv.at[t], (g, beside(0, 1))
        )

    def target(t):
        return (ahead(DISTANCES[(first + t) % 4]), f)

    def value_copy(t, c):
        return remote(
            value_msg.at[t % 2, c],
            value_got.at[t, c],
            value_send.at[t, c],
            value_recv.at[t, c],
            target(t),
        )

    def output_copy(t, c):
        return remote(
            output_msg.at[t % 2, c],
            output_got.at[t, c],
            output_send.at[t, c],
            output_recv.at[t, c],
            target(t),
        )

    def into_relay(p):
        c = chunk_at(p) if values_lead else p
        held, sent = (value_msg, value_send) if values_lead else (output_msg, output_send)
        return remote(
            held.at[slow_step % 2, c],
            relay.at[p],
            sent.at[slow_step, c],
            relay_recv.at[p],
            (behind(RELAY), f),
        )

    def from_relay(p):
        c = chunk_at(p) if values_lead else p
        got, landed = (value_got, value_recv) if values_lead else (output_got, output_recv)
        return remote(
            relay.at[p],
            got.at[slow_step, c],
            relay_send.at[p],
            landed.at[slow_step, c],
            (behind(RELAY), f),
        )

    def side_step(i):
        return (i - first) % steps

    def goes_aside(i):
        return lax.rem(g, 4) >= 3 - i

    def into_side(i, p):
        t = side_step(i)
        values = t >= 2
        c = chunk_at(p) if values else p
        held, sent = (value_msg, value_send) if values else (output_msg, output_send)
        return remote(
            held.at[t % 2, c],
            (side_one, side_two)[i].at[p],
            sent.at[t, c],
            side_recv.at[i, p],
            (behind(3 - i), f),
        )

    def from_side(i, p):
        t = side_step(i)
        values = t >= 2
        c = chunk_at(p) if values else p
        got, landed = (value_got, value_recv) if values else (output_got, output_recv)
        return remote(
            (side_one, side_two)[i].at[p],
            got.at[t, c],
            side_send.at[i, p],
            landed.at[t, c],
            (ahead(4), f),
        )

    def at_side(i, body):
        @pl.when(lax.rem(g, 4) <= i)
        def _():
            each(body, 0, SIDE)

    def pass_side(i):
        def one(p):
            into_side(i, p).wait_recv()
            from_side(i, p).start()

        at_side(i, one)

    def pass_relay():
        def one(p):
            into_relay(p).wait_recv()
            from_relay(p).start()

        each(one, 0, detour)

    def send_message(t, copy, values, p):
        if t == slow_step and values == values_lead:

            @pl.when(p < detour)
            def _():
                into_relay(p).start()

            @pl.when(p >= detour)
            def _():
                copy.start()

        elif (first + t) % 4 < 2 and values == (t >= 2):
            i = (first + t) % 4
            aside = jnp.logical_and(goes_aside(i), p < SIDE)

            @pl.when(aside)
            def _():
                into_side(i, p).start()

            @pl.when(jnp.logical_not(aside))
            def _():
                copy.start()

        else:
            copy.start()

    def span(t, values, point):
        marks = PACE[(first + t) % 4] if t + 1 < steps else (2 * peers, 2 * peers)
        marks = (0, *marks, 2 * peers)
        shift = 0 if values == (t >= 2) else peers
        return tuple(min(max(m - shift, 0), peers) for m in marks[point : point + 2])

    def send_value(t, p):
        send_message(t, value_copy(t, chunk_at(p)), True, p)

    def send_output(t, p):
        send_message(t, output_copy(t, p), False, p)

    def send_later(t, point):
        each(lambda p: send_output(t, p), *span(t, False, point))
        each(lambda p: send_value(t, p), *span(t, True, point))

    def send_prompt(t, values, p):
        send = send_value if values else send_output
        if span(t, values, 0)[1] == peers:
            send(t, p)
        elif span(t, values, 0)[1] > 0:

            @pl.when(p < span(t, values, 0)[1])
            def _():
                send(t, p)

    def mass_copy(t):
        return remote(
            mass_msg.at[t], mass_got.at[t], mass_send.at[t], mass_recv.at[t], target(t)
        )

    def each(body, start=0, stop=peers):
        def run(i, carry):
            body(i)
            return carry

        lax.fori_loop(start, stop, run, 0)

    for copy in loads():
        copy.start()
    own_x.start()
    own_cot.start()

    barrier = pltpu.get_barrier_semaphore()
    for k in range(1, peers):
        pl.semaphore_signal(barrier, inc=1, device_id=(g, peer(k)), device_id_type=MESH)
    for distance in DISTANCES:
        pl.semaphore_signal(barrier, inc=1, device_id=(behind(distance), f), device_id_type=MESH)
    pl.semaphore_signal(barrier, inc=1, device_id=(ahead(RELAY), f), device_id_type=MESH)
    for distance in (2, 3):
        pl.semaphore_signal(barrier, inc=1, device_id=(ahead(distance), f), device_id_type=MESH)
    pl.semaphore_wait(barrier, peers + len(DISTANCES) + 2)

    each(lambda k: x_copy(0, k).start(), 1)
    cot_lead(0)
    each(lambda k: x_copy(1, k).start(), 1)

    for copy in loads():
        copy.wait()

    def widen(c):
        value_w[c] = value_msg[1, c].astype(F32)
        output_w[c] = output_msg[1, c].astype(F32)

    each(widen)
    cot_pass(0)

    spread = (
        lax.rem(lax.broadcasted_iota(jnp.int32, (batch, positions), 0), positions)
        == lax.broadcasted_iota(jnp.int32, (batch, positions), 1)
    ).astype(BF16)
    same = (
        lax.broadcasted_iota(jnp.int32, (batch, batch), 0) // positions
        == lax.broadcasted_iota(jnp.int32, (batch, batch), 1) // positions
    )
    for h in range(heads):
        logits = bias[f * heads + h]
        weights = jnp.exp(logits - jnp.max(logits, axis=-1, keepdims=True))
        weights = (weights / jnp.sum(weights, axis=-1, keepdims=True)).astype(BF16)
        for held, dims in ((mix, ((1,), (0,))), (mix_turned, ((1,), (1,)))):
            tall = lax.dot_general(spread, weights, (dims, ((), ())), preferred_element_type=F32)
            wide = lax.dot_general(
                tall.astype(BF16), spread, (((1,), (1,)), ((), ())), preferred_element_type=F32
            )
            held[h] = jnp.where(same, wide, 0.0).astype(BF16)

    head_of = lax.broadcasted_iota(jnp.int32, (batch, v_cols), 1) // head_size

    def by_heads(weights, block):
        result = jnp.zeros((batch, v_cols), F32)
        for h in range(heads):
            product = jnp.dot(weights[h], block, preferred_element_type=F32)
            result = jnp.where(head_of == h, product, result)
        return result.astype(BF16)

    mass = mass_in[...]
    own_x.wait()
    own_cot.wait()
    each(lambda k: x_copy(0, k).wait_recv(), 1)

    for t in range(steps):
        slot = t % 2
        inverse[...] = 1.0 / mass

        if t == 1:
            each(lambda k: x_copy(1, k).wait_recv(), 1)
        x_turned[...] = x_cols[t].reshape(batch, x_width).T

        def values_of(j, half, t=t):
            c = beside(j, half)
            if t >= 2:
                value_copy(t - 2, c).wait_recv()
                value_w[c] = value_w[c] + value_got[t - 2, c].astype(F32)
            effective = (value_w[c] * inverse[0:1, 0:v_cols]).astype(BF16)
            product = jnp.dot(
                x_cols[t].reshape(batch, x_width), effective, preferred_element_type=F32
            )
            return (product * scale_in).astype(BF16)

        def send_part(j, t=t, values_of=values_of):
            part[j, 0] = values_of(j, 0)
            part[j, 1] = values_of(j, 1)
            part_copy(t, j).start()

        def forward(t=t, values_of=values_of, send_part=send_part):
            each(send_part, 1, row)
            part_got[t, 0, 0] = values_of(0, 0)
            part_got[t, 0, 1] = values_of(0, 1)

        def cross(t=t):
            each(lambda j: part_copy(t, j).wait(), 1, row)
            summed = part_got[t, 0, 1].astype(F32)
            for j in range(1, row):
                summed = summed + part_got[t, j, 1].astype(F32)
            across[...] = summed.astype(BF16)
            across_copy(t).start()

        def pass_dvalues(t=t):
            dv_copy(t, 0).wait_recv()
            each(lambda j: dv_copy(t, row + j).start(), 1, row)

        def add_dmixed(i, t=t):
            c = i
            if t >= 2:
                if t - 2 == slow_step and not values_lead:
                    c = lax.rem(i + detour, peers)
                output_copy(t - 2, c).wait_recv()
                output_w[c] = output_w[c] + output_got[t - 2, c].astype(F32)
            effective = (output_w[c] * inverse[0:1, 0:o_cols]).astype(BF16)
            cot = cot_all[t, :, :, pl.ds(pl.multiple_of(c * o_cols, o_cols), o_cols)]
            total[...] += lax.dot_general(
                cot.reshape(batch, o_cols),
                effective,
                (((1,), (1,)), ((), ())),
                preferred_element_type=F32,
            )

        def backward(t=t, add_dmixed=add_dmixed):
            each(lambda j: cot_copy(t, j).wait_recv(), 1, row)
            each(lambda j: cot_copy(t, row + j).wait_recv(), 1, row)
            total[...] = jnp.zeros_like(total)
            each(add_dmixed)
            dmixed = (total[...] * scale_mid).astype(BF16)
            dvalues_all[t, f] = by_heads(mix_turned, dmixed)
            dv_copy(t, 0).start()
            each(lambda j: dv_copy(t, j).start(), 1, row)

        def update_output(c, t=t, slot=slot):
            cot = cot_all[t, :, :, pl.ds(pl.multiple_of(c * o_cols, o_cols), o_cols)]
            grad = jnp.dot(
                mixed_turned[...], cot.reshape(batch, o_cols), preferred_element_type=F32
            )
            half = 0.5 * output_w[c] - (0.25 * scale_mid) * grad
            output_w[c] = half
            if t >= 2:
                output_copy(t - 2, c).wait_send()
            output_msg[slot, c] = half.astype(BF16)
            send_prompt(t, False, c)

        def outputs(t=t, update_output=update_output):
            summed = part_got[t, 0, 0].astype(F32)
            for j in range(1, row):
                summed = summed + part_got[t, j, 0].astype(F32)
            across_copy(t).wait()
            summed = summed + across_got[t].astype(F32)
            mixed_turned[...] = by_heads(mix, summed.astype(BF16)).T
            each(update_output)

        def update_value(p, t=t, slot=slot):
            c = chunk_at(p)
            grad = jnp.dot(x_turned[...], dvalues_all[t, c], preferred_element_type=F32)
            half = 0.5 * value_w[c] - (0.25 * scale_in) * grad
            value_w[c] = half
            if t >= 2:
                value_copy(t - 2, c).wait_send()
            value_msg[slot, c] = half.astype(BF16)
            send_prompt(t, True, p)

        def update_other(p, t=t, update_value=update_value):
            dv_copy(t, row * lax.rem(p, 2) + row - 1 - p // 2).wait_recv()
            update_value(p)

        def values(t=t, update_value=update_value, update_other=update_other):
            each(update_other, 0, peers - 2)
            each(update_value, peers - 2)

        half_mass = mass * 0.5
        if t < 2:
            forward()
            backward()
            if t >= 1:
                send_later(t - 1, 1)
            cross()
            pass_dvalues()
        else:
            backward()
            forward()
            send_later(t - 1, 1)
            pass_dvalues()
            cross()
        if t + 1 < steps:
            cot_lead(t + 1)
        if t >= 1:
            send_later(t - 1, 2)
        if t < 2:
            outputs()
            values()
        else:
            values()
            outputs()
        if t + 1 < steps:
            cot_pass(t + 1)
        for earlier in range(steps):
            if t == min(earlier + 1, steps - 1):
                if earlier == slow_step:
                    pass_relay()
                for i in range(2):
                    if earlier == side_step(i):
                        pass_side(i)
        mass_msg[t] = half_mass.astype(BF16)
        mass_copy(t).start()
        mass = half_mass
        if t >= 1:
            mass_copy(t - 1).wait_recv()
            mass = mass + mass_got[t - 1].astype(F32)

    last = steps - 1
    mass_copy(last).wait_recv()
    mass = mass + mass_got[last].astype(F32)
    mass_out[...] = mass
    inverse[...] = 1.0 / mass

    def value_store(c):
        return pltpu.make_async_copy(
            value_msg.at[0, c],
            value_out.at[0, :, pl.ds(pl.multiple_of(c * v_cols, v_cols), v_cols)],
            load_sem.at[0, c],
        )

    def output_store(c):
        return pltpu.make_async_copy(
            output_msg.at[0, c],
            output_out.at[0, :, pl.ds(pl.multiple_of(c * o_cols, o_cols), o_cols)],
            load_sem.at[1, c],
        )

    def finish_value(i):
        p = lax.rem(i + detour, peers) if values_lead else i
        c = chunk_at(p)
        value_copy(last - 1, c).wait()
        value_copy(last, c).wait_recv()
        result = (
            value_w[c] + value_got[last - 1, c].astype(F32) + value_got[last, c].astype(F32)
        )
        value_msg[0, c] = (result * inverse[0:1, 0:v_cols]).astype(BF16)
        value_store(c).start()

    def finish_output(c):
        output_copy(last - 1, c).wait()
        output_copy(last, c).wait_recv()
        result = (
            output_w[c] + output_got[last - 1, c].astype(F32) + output_got[last, c].astype(F32)
        )
        output_msg[0, c] = (result * inverse[0:1, 0:o_cols]).astype(BF16)
        output_store(c).start()

    each(finish_value)
    each(finish_output)

    def settle(k):
        x_copy(0, k).wait_send()
        x_copy(1, k).wait_send()

    each(settle, 1)

    def settle_row(j):
        for t in range(steps):
            cot_copy(t, j).wait_send()
            cot_copy(t, row + j).wait_send()
            dv_copy(t, j).wait_send()
            dv_copy(t, row + j).wait_send()

    each(settle_row, 1, row)
    for t in range(steps):
        cot_copy(t, 0).wait_send()
        dv_copy(t, 0).wait_send()

    each(lambda p: from_relay(p).wait_send(), 0, detour)
    at_side(0, lambda p: from_side(0, p).wait_send())
    at_side(1, lambda p: from_side(1, p).wait_send())

    def settle_chunk(c):
        value_copy(last, c).wait_send()
        output_copy(last, c).wait_send()
        value_store(c).wait()
        output_store(c).wait()

    each(settle_chunk)
    for t in range(steps):
        mass_copy(t).wait_send()


def run_window(first, inputs, cotangent, value_weight, output_weight, mass, bias):
    groups = lax.axis_size("group")
    peers = lax.axis_size("fsdp")
    _, steps, positions, width = inputs.shape
    rows, inner = value_weight.shape[1:]
    own_inner = output_weight.shape[1]
    heads = bias.shape[0] // peers
    head_size = own_inner // heads
    batch = positions * peers
    o_cols = width // peers
    lanes = mass.shape[1]
    dma = pltpu.SemaphoreType.DMA
    hbm = pl.BlockSpec(memory_space=pl.ANY)
    vmem = pl.BlockSpec(memory_space=pltpu.VMEM)

    def chunk_of(step):
        return (rows, own_inner) if step % steps >= 2 else (own_inner, o_cols)

    relay_shape = (max(max(DETOUR[first]), 1), *chunk_of(3 - first))
    sizes = (groups, peers, steps, positions, heads, head_size)
    return pl.pallas_call(
        functools.partial(window_kernel, first, sizes),
        out_shape=(
            jax.ShapeDtypeStruct(value_weight.shape, BF16),
            jax.ShapeDtypeStruct(output_weight.shape, BF16),
            jax.ShapeDtypeStruct(mass.shape, F32),
        ),
        in_specs=[hbm, hbm, hbm, hbm, vmem, vmem],
        out_specs=(hbm, hbm, vmem),
        scratch_shapes=[
            pltpu.VMEM((steps, peers, positions, rows), BF16),
            pltpu.VMEM((rows, batch), BF16),
            pltpu.VMEM((steps, peers, positions, width), BF16),
            pltpu.VMEM((peers, rows, own_inner), F32),
            pltpu.VMEM((peers, own_inner, o_cols), F32),
            pltpu.VMEM((2, peers, rows, own_inner), BF16),
            pltpu.VMEM((2, peers, own_inner, o_cols), BF16),
            pltpu.VMEM((steps, *mass.shape), BF16),
            pltpu.VMEM((steps, peers, rows, own_inner), BF16),
            pltpu.VMEM((steps, peers, own_inner, o_cols), BF16),
            pltpu.VMEM((steps, *mass.shape), BF16),
            pltpu.VMEM((peers // 2, 2, batch, own_inner), BF16),
            pltpu.VMEM((steps, peers // 2, 2, batch, own_inner), BF16),
            pltpu.VMEM((batch, own_inner), BF16),
            pltpu.VMEM((steps, batch, own_inner), BF16),
            pltpu.VMEM(relay_shape, BF16),
            pltpu.VMEM((SIDE, *chunk_of(-first)), BF16),
            pltpu.VMEM((SIDE, *chunk_of(1 - first)), BF16),
            pltpu.VMEM((steps, peers, batch, own_inner), BF16),
            pltpu.VMEM((heads, batch, batch), BF16),
            pltpu.VMEM((heads, batch, batch), BF16),
            pltpu.VMEM((own_inner, batch), BF16),
            pltpu.VMEM((batch, own_inner), F32),
            pltpu.VMEM(mass.shape, F32),
            dma((2, peers)),
            dma((2,)),
            dma((2, peers)),
            dma((2, peers)),
            dma((steps, peers)),
            dma((steps, peers)),
            dma((steps, peers)),
            dma((steps, peers)),
            dma((steps, peers)),
            dma((steps, peers)),
            dma((steps, peers)),
            dma((steps, peers)),
            dma((steps, peers)),
            dma((steps, peers)),
            dma((steps,)),
            dma((steps,)),
            dma((steps,)),
            dma((steps,)),
            dma((peers,)),
            dma((peers,)),
            dma((2, peers)),
            dma((2, peers)),
        ],
        compiler_params=pltpu.CompilerParams(
            collective_id=first, has_side_effects=True, vmem_limit_bytes=63 << 20
        ),
        name="window",
    )(inputs, cotangent, value_weight, output_weight, mass, bias)


def on_device(
    inputs, cotangent, value_weight, output_weight, push_weight, position_bias, step_index
):
    mass = jnp.broadcast_to(push_weight[:, None], (16, 512))
    value_out, output_out, mass = lax.switch(
        step_index[0] % 4,
        [functools.partial(run_window, first) for first in range(4)],
        inputs,
        cotangent,
        value_weight,
        output_weight,
        mass,
        position_bias,
    )
    return (value_out, output_out, mass[0, :1])


def solution(mesh):
    placed = (
        P("group", None, "fsdp", None),
        P("group", None, "fsdp", None),
        P("group", "fsdp", None),
        P("group", "fsdp", None),
        P("group"),
        P(),
        P(),
    )
    return jax.shard_map(
        on_device,
        mesh=mesh,
        in_specs=placed,
        out_specs=(P("group", "fsdp", None), P("group", "fsdp", None), P("group")),
        check_vma=False,
    )
```

```python
import functools
import math

import jax
import jax.numpy as jnp
from jax import lax
from jax.experimental import pallas as pl
from jax.experimental.pallas import tpu as pltpu
from jax.sharding import PartitionSpec as P

DISTANCES = (1, 2, 4, 8)
RELAY = 12
SIDE = 8
PACE = (((4, 6), (2, 3), (16, 16), (16, 16)), ((4, 6), (1, 2), (16, 16), (16, 16)), ((16, 16), (16, 16), (16, 16), (16, 16)), ((16, 16), (1, 2), (16, 16), (16, 16)))
COT_OVER_Y = (2, 2, 2, 1)
DV_OVER_Y = False
DETOUR = ((4, 4), (4, 4), (5, 5), (4, 4))
MESH = pl.DeviceIdType.MESH
F32 = jnp.float32
BF16 = jnp.bfloat16


def window_kernel(
    first,
    sizes,
    inputs,
    cotangent,
    value_in,
    output_in,
    mass_in,
    bias,
    value_out,
    output_out,
    mass_out,
    x_cols,
    x_turned,
    cot_all,
    value_w,
    output_w,
    value_msg,
    output_msg,
    mass_msg,
    value_got,
    output_got,
    mass_got,
    part,
    part_got,
    across,
    across_got,
    relay,
    side_one,
    side_two,
    dvalues_all,
    mix,
    mix_turned,
    mixed_turned,
    total,
    inverse,
    load_sem,
    own_sem,
    x_send,
    x_recv,
    cot_send,
    cot_recv,
    part_send,
    part_recv,
    dv_send,
    dv_recv,
    value_send,
    value_recv,
    output_send,
    output_recv,
    mass_send,
    mass_recv,
    across_send,
    across_recv,
    relay_send,
    relay_recv,
    side_send,
    side_recv,
):
    groups, peers, steps, positions, heads, head_size = sizes
    batch = peers * positions
    v_cols = value_w.shape[2]
    o_cols = output_w.shape[2]
    x_width = x_cols.shape[3]
    scale_in = 1.0 / math.sqrt(x_width * peers)
    scale_mid = 1.0 / math.sqrt(v_cols * peers)
    g = lax.axis_index("group")
    f = lax.axis_index("fsdp")
    row = peers // 2
    y_half = f // row
    x_place = lax.rem(f, row)
    slow_step = (3 - first) % steps
    detour = DETOUR[first][0] + (DETOUR[first][1] - DETOUR[first][0]) * lax.rem(g // 2, 2)
    values_lead = slow_step >= 2

    def peer(k):
        return lax.rem(f + k, peers)

    def beside(j, s=0):
        return lax.rem(y_half + s, 2) * row + lax.rem(x_place + j, row)

    def chunk_at(p):
        return beside(lax.rem(p // 2 + 1, row), lax.rem(p, 2))

    def ahead(distance):
        return lax.rem(g + distance, groups)

    def behind(distance):
        return lax.rem(g + groups - distance, groups)

    def remote(src, dst, send, recv, device):
        return pltpu.make_async_remote_copy(
            src_ref=src,
            dst_ref=dst,
            send_sem=send,
            recv_sem=recv,
            device_id=device,
            device_id_type=MESH,
        )

    def loads():
        for c in range(peers):
            yield pltpu.make_async_copy(
                value_in.at[0, :, pl.ds(c * v_cols, v_cols)], value_msg.at[1, c], load_sem.at[0, c]
            )
            yield pltpu.make_async_copy(
                output_in.at[0, :, pl.ds(c * o_cols, o_cols)],
                output_msg.at[1, c],
                load_sem.at[1, c],
            )

    def columns_of(p):
        return pl.ds(pl.multiple_of(p * x_width, x_width), x_width)

    own_x = pltpu.make_async_copy(
        inputs.at[0, :, :, columns_of(f)], x_cols.at[:, f], own_sem.at[0]
    )
    own_cot = pltpu.make_async_copy(cotangent.at[0], cot_all.at[:, f], own_sem.at[1])

    def x_copy(late, k):
        when = pl.ds(1, steps - 1) if late else pl.ds(0, 1)
        return remote(
            inputs.at[0, when, :, columns_of(peer(k))],
            x_cols.at[when, f],
            x_send.at[late, k],
            x_recv.at[late, k],
            (g, peer(k)),
        )

    def second(held, t, j, send, recv, over_y):
        block, to = beside(0, 1), beside(j)
        if j == 2 and over_y:
            block, to = beside(2), beside(0, 1)
        return remote(
            held.at[t, block],
            held.at[t, block],
            send.at[t, row + j],
            recv.at[t, row + j],
            (g, to),
        )

    def cot_second(t, j):
        return second(cot_all, t, j, cot_send, cot_recv, t < COT_OVER_Y[first])

    def dv_second(t, j):
        return second(dvalues_all, t, j, dv_send, dv_recv, DV_OVER_Y)

    def cot_first(t, k):
        to = beside(k) if not isinstance(k, int) or k else beside(0, 1)
        return remote(
            cotangent.at[0, t], cot_all.at[t, f], cot_send.at[t, k], cot_recv.at[t, k], (g, to)
        )

    def cot_lead(t):
        cot_first(t, 0).start()
        each(lambda j: cot_first(t, j).start(), 1, row)

    def cot_pass(t):
        cot_first(t, 0).wait_recv()
        cot_second(t, 1).start()
        cot_second(t, 3).start()
        cot_first(t, 2).wait_recv()
        cot_second(t, 2).start()

    def dv_first(t, k):
        to = beside(k) if not isinstance(k, int) or k else beside(0, 1)
        return remote(
            dvalues_all.at[t, f],
            dvalues_all.at[t, f],
            dv_send.at[t, k],
            dv_recv.at[t, k],
            (g, to),
        )

    def part_copy(t, j):
        return remote(
            part.at[j],
            part_got.at[t, j],
            part_send.at[t, j],
            part_recv.at[t, j],
            (g, beside(j)),
        )

    def across_copy(t):
        return remote(
            across, across_got.at[t], across_send.at[t], across_recv.at[t], (g, beside(0, 1))
        )

    def target(t):
        return (ahead(DISTANCES[(first + t) % 4]), f)

    def value_copy(t, c):
        return remote(
            value_msg.at[t % 2, c],
            value_got.at[t, c],
            value_send.at[t, c],
            value_recv.at[t, c],
            target(t),
        )

    def output_copy(t, c):
        return remote(
            output_msg.at[t % 2, c],
            output_got.at[t, c],
            output_send.at[t, c],
            output_recv.at[t, c],
            target(t),
        )

    def into_relay(p):
        c = chunk_at(p) if values_lead else p
        held, sent = (value_msg, value_send) if values_lead else (output_msg, output_send)
        return remote(
            held.at[slow_step % 2, c],
            relay.at[p],
            sent.at[slow_step, c],
            relay_recv.at[p],
            (behind(RELAY), f),
        )

    def from_relay(p):
        c = chunk_at(p) if values_lead else p
        got, landed = (value_got, value_recv) if values_lead else (output_got, output_recv)
        return remote(
            relay.at[p],
            got.at[slow_step, c],
            relay_send.at[p],
            landed.at[slow_step, c],
            (behind(RELAY), f),
        )

    def side_step(i):
        return (i - first) % steps

    def goes_aside(i):
        return lax.rem(g, 4) >= 3 - i

    def into_side(i, p):
        t = side_step(i)
        values = t >= 2
        c = chunk_at(p) if values else p
        held, sent = (value_msg, value_send) if values else (output_msg, output_send)
        return remote(
            held.at[t % 2, c],
            (side_one, side_two)[i].at[p],
            sent.at[t, c],
            side_recv.at[i, p],
            (behind(3 - i), f),
        )

    def from_side(i, p):
        t = side_step(i)
        values = t >= 2
        c = chunk_at(p) if values else p
        got, landed = (value_got, value_recv) if values else (output_got, output_recv)
        return remote(
            (side_one, side_two)[i].at[p],
            got.at[t, c],
            side_send.at[i, p],
            landed.at[t, c],
            (ahead(4), f),
        )

    def at_side(i, body):
        @pl.when(lax.rem(g, 4) <= i)
        def _():
            each(body, 0, SIDE)

    def pass_side(i):
        def one(p):
            into_side(i, p).wait_recv()
            from_side(i, p).start()

        at_side(i, one)

    def pass_relay():
        def one(p):
            into_relay(p).wait_recv()
            from_relay(p).start()

        each(one, 0, detour)

    def send_message(t, copy, values, p):
        if t == slow_step and values == values_lead:

            @pl.when(p < detour)
            def _():
                into_relay(p).start()

            @pl.when(p >= detour)
            def _():
                copy.start()

        elif (first + t) % 4 < 2 and values == (t >= 2):
            i = (first + t) % 4
            aside = jnp.logical_and(goes_aside(i), p < SIDE)

            @pl.when(aside)
            def _():
                into_side(i, p).start()

            @pl.when(jnp.logical_not(aside))
            def _():
                copy.start()

        else:
            copy.start()

    def span(t, values, point):
        marks = PACE[first][(first + t) % 4] if t + 1 < steps else (2 * peers, 2 * peers)
        marks = (0, *marks, 2 * peers)
        shift = 0 if values == (t >= 2) else peers
        return tuple(min(max(m - shift, 0), peers) for m in marks[point : point + 2])

    def send_value(t, p):
        send_message(t, value_copy(t, chunk_at(p)), True, p)

    def send_output(t, p):
        send_message(t, output_copy(t, p), False, p)

    def send_later(t, point):
        each(lambda p: send_output(t, p), *span(t, False, point))
        each(lambda p: send_value(t, p), *span(t, True, point))

    def send_prompt(t, values, p):
        send = send_value if values else send_output
        if span(t, values, 0)[1] == peers:
            send(t, p)
        elif span(t, values, 0)[1] > 0:

            @pl.when(p < span(t, values, 0)[1])
            def _():
                send(t, p)

    def mass_copy(t):
        return remote(
            mass_msg.at[t], mass_got.at[t], mass_send.at[t], mass_recv.at[t], target(t)
        )

    def each(body, start=0, stop=peers):
        def run(i, carry):
            body(i)
            return carry

        lax.fori_loop(start, stop, run, 0)

    for copy in loads():
        copy.start()
    own_x.start()
    own_cot.start()

    barrier = pltpu.get_barrier_semaphore()
    for k in range(1, peers):
        pl.semaphore_signal(barrier, inc=1, device_id=(g, peer(k)), device_id_type=MESH)
    for distance in DISTANCES:
        pl.semaphore_signal(barrier, inc=1, device_id=(behind(distance), f), device_id_type=MESH)
    pl.semaphore_signal(barrier, inc=1, device_id=(ahead(RELAY), f), device_id_type=MESH)
    for distance in (2, 3):
        pl.semaphore_signal(barrier, inc=1, device_id=(ahead(distance), f), device_id_type=MESH)
    pl.semaphore_wait(barrier, peers + len(DISTANCES) + 2)

    each(lambda k: x_copy(0, k).start(), 1)
    cot_lead(0)

    for copy in loads():
        copy.wait()

    def widen(c):
        value_w[c] = value_msg[1, c].astype(F32)
        output_w[c] = output_msg[1, c].astype(F32)

    each(widen)
    cot_pass(0)

    spread = (
        lax.rem(lax.broadcasted_iota(jnp.int32, (batch, positions), 0), positions)
        == lax.broadcasted_iota(jnp.int32, (batch, positions), 1)
    ).astype(BF16)
    same = (
        lax.broadcasted_iota(jnp.int32, (batch, batch), 0) // positions
        == lax.broadcasted_iota(jnp.int32, (batch, batch), 1) // positions
    )
    for h in range(heads):
        logits = bias[f * heads + h]
        weights = jnp.exp(logits - jnp.max(logits, axis=-1, keepdims=True))
        weights = (weights / jnp.sum(weights, axis=-1, keepdims=True)).astype(BF16)
        for held, dims in ((mix, ((1,), (0,))), (mix_turned, ((1,), (1,)))):
            tall = lax.dot_general(spread, weights, (dims, ((), ())), preferred_element_type=F32)
            wide = lax.dot_general(
                tall.astype(BF16), spread, (((1,), (1,)), ((), ())), preferred_element_type=F32
            )
            held[h] = jnp.where(same, wide, 0.0).astype(BF16)

    head_of = lax.broadcasted_iota(jnp.int32, (batch, v_cols), 1) // head_size

    def by_heads(weights, block):
        result = jnp.zeros((batch, v_cols), F32)
        for h in range(heads):
            product = jnp.dot(weights[h], block, preferred_element_type=F32)
            result = jnp.where(head_of == h, product, result)
        return result.astype(BF16)

    mass = mass_in[...]
    own_x.wait()
    own_cot.wait()
    each(lambda k: x_copy(0, k).wait_recv(), 1)

    for t in range(steps):
        slot = t % 2
        inverse[...] = 1.0 / mass

        if t == 1:
            each(lambda k: x_copy(1, k).wait_recv(), 1)
        x_turned[...] = x_cols[t].reshape(batch, x_width).T

        def values_of(j, half, t=t):
            c = beside(j, half)
            if t >= 2:
                value_copy(t - 2, c).wait_recv()
                value_w[c] = value_w[c] + value_got[t - 2, c].astype(F32)
            effective = (value_w[c] * inverse[0:1, 0:v_cols]).astype(BF16)
            product = jnp.dot(
                x_cols[t].reshape(batch, x_width), effective, preferred_element_type=F32
            )
            return (product * scale_in).astype(BF16)

        def send_part(j, t=t, values_of=values_of):
            part[j, 0] = values_of(j, 0)
            part[j, 1] = values_of(j, 1)
            part_copy(t, j).start()

        def forward(t=t, values_of=values_of, send_part=send_part):
            each(send_part, 1, row)
            part_got[t, 0, 0] = values_of(0, 0)
            part_got[t, 0, 1] = values_of(0, 1)

        def cross(t=t):
            each(lambda j: part_copy(t, j).wait(), 1, row)
            summed = part_got[t, 0, 1].astype(F32)
            for j in range(1, row):
                summed = summed + part_got[t, j, 1].astype(F32)
            across[...] = summed.astype(BF16)
            across_copy(t).start()

        def pass_dvalues(t=t):
            dv_first(t, 0).wait_recv()
            dv_second(t, 1).start()
            dv_second(t, 3).start()
            dv_first(t, 2).wait_recv()
            dv_second(t, 2).start()

        def add_dmixed(i, t=t):
            c = i
            if t >= 2:
                if t - 2 == slow_step and not values_lead:
                    c = lax.rem(i + detour, peers)
                output_copy(t - 2, c).wait_recv()
                output_w[c] = output_w[c] + output_got[t - 2, c].astype(F32)
            effective = (output_w[c] * inverse[0:1, 0:o_cols]).astype(BF16)
            cot = cot_all[t, :, :, pl.ds(pl.multiple_of(c * o_cols, o_cols), o_cols)]
            total[...] += lax.dot_general(
                cot.reshape(batch, o_cols),
                effective,
                (((1,), (1,)), ((), ())),
                preferred_element_type=F32,
            )

        def backward(t=t, add_dmixed=add_dmixed):
            for j in (1, 3):
                cot_first(t, j).wait_recv()
            for j in (1, 2, 3):
                cot_second(t, j).wait_recv()
            total[...] = jnp.zeros_like(total)
            each(add_dmixed)
            dmixed = (total[...] * scale_mid).astype(BF16)
            dvalues_all[t, f] = by_heads(mix_turned, dmixed)
            dv_first(t, 0).start()
            each(lambda j: dv_first(t, j).start(), 1, row)

        def update_output(c, t=t, slot=slot):
            cot = cot_all[t, :, :, pl.ds(pl.multiple_of(c * o_cols, o_cols), o_cols)]
            grad = jnp.dot(
                mixed_turned[...], cot.reshape(batch, o_cols), preferred_element_type=F32
            )
            half = 0.5 * output_w[c] - (0.25 * scale_mid) * grad
            output_w[c] = half
            if t >= 2:
                output_copy(t - 2, c).wait_send()
            output_msg[slot, c] = half.astype(BF16)
            send_prompt(t, False, c)

        def outputs(t=t, update_output=update_output):
            summed = part_got[t, 0, 0].astype(F32)
            for j in range(1, row):
                summed = summed + part_got[t, j, 0].astype(F32)
            across_copy(t).wait()
            summed = summed + across_got[t].astype(F32)
            mixed_turned[...] = by_heads(mix, summed.astype(BF16)).T
            each(update_output)

        def update_value(p, t=t, slot=slot):
            c = chunk_at(p)
            grad = jnp.dot(x_turned[...], dvalues_all[t, c], preferred_element_type=F32)
            half = 0.5 * value_w[c] - (0.25 * scale_in) * grad
            value_w[c] = half
            if t >= 2:
                value_copy(t - 2, c).wait_send()
            value_msg[slot, c] = half.astype(BF16)
            send_prompt(t, True, p)

        def update_other(p, t=t, update_value=update_value):
            @pl.when(p != 2)
            def _():
                dv_first(t, row * lax.rem(p, 2) + row - 1 - p // 2).wait_recv()

            update_value(p)

        def values(t=t, update_value=update_value, update_other=update_other):
            each(update_other, 0, peers - 2)
            each(update_value, peers - 2)

        half_mass = mass * 0.5
        if t < 2:
            forward()
            backward()
            if t >= 1:
                send_later(t - 1, 1)
            cross()
            pass_dvalues()
        elif first != 3 and (first + t - 2) % 4 != 2:
            forward()
            backward()
            send_later(t - 1, 1)
            cross()
            pass_dvalues()
        else:
            backward()
            forward()
            send_later(t - 1, 1)
            pass_dvalues()
            cross()
        if t == 0:
            each(lambda k: x_copy(1, k).start(), 1)
        if t + 1 < steps:
            cot_lead(t + 1)
        if t >= 1:
            send_later(t - 1, 2)
        if t < 2:
            outputs()
        else:
            values()
        if t + 1 < steps:
            cot_pass(t + 1)
        if t < 2:
            values()
        else:
            outputs()
        for earlier in range(steps):
            if t == min(earlier + 1, steps - 1):
                if earlier == slow_step:
                    pass_relay()
                for i in range(2):
                    if earlier == side_step(i):
                        pass_side(i)
        mass_msg[t] = half_mass.astype(BF16)
        mass_copy(t).start()
        mass = half_mass
        if t >= 1:
            mass_copy(t - 1).wait_recv()
            mass = mass + mass_got[t - 1].astype(F32)

    last = steps - 1
    mass_copy(last).wait_recv()
    mass = mass + mass_got[last].astype(F32)
    mass_out[...] = mass
    inverse[...] = 1.0 / mass

    def value_store(c):
        return pltpu.make_async_copy(
            value_msg.at[0, c],
            value_out.at[0, :, pl.ds(pl.multiple_of(c * v_cols, v_cols), v_cols)],
            load_sem.at[0, c],
        )

    def output_store(c):
        return pltpu.make_async_copy(
            output_msg.at[0, c],
            output_out.at[0, :, pl.ds(pl.multiple_of(c * o_cols, o_cols), o_cols)],
            load_sem.at[1, c],
        )

    def finish_value(i):
        p = lax.rem(i + detour, peers) if values_lead else i
        c = chunk_at(p)
        value_copy(last - 1, c).wait()
        value_copy(last, c).wait_recv()
        result = (
            value_w[c] + value_got[last - 1, c].astype(F32) + value_got[last, c].astype(F32)
        )
        value_msg[0, c] = (result * inverse[0:1, 0:v_cols]).astype(BF16)
        value_store(c).start()

    def finish_output(c):
        output_copy(last - 1, c).wait()
        output_copy(last, c).wait_recv()
        result = (
            output_w[c] + output_got[last - 1, c].astype(F32) + output_got[last, c].astype(F32)
        )
        output_msg[0, c] = (result * inverse[0:1, 0:o_cols]).astype(BF16)
        output_store(c).start()

    if first == 3:
        each(finish_value)
        each(finish_output)
    else:
        each(finish_output)
        each(finish_value)

    def settle(k):
        x_copy(0, k).wait_send()
        x_copy(1, k).wait_send()

    each(settle, 1)

    for t in range(steps):
        for j in range(row):
            cot_first(t, j).wait_send()
            dv_first(t, j).wait_send()
        for j in range(1, row):
            cot_second(t, j).wait_send()
            dv_second(t, j).wait_send()

    each(lambda p: from_relay(p).wait_send(), 0, detour)
    at_side(0, lambda p: from_side(0, p).wait_send())
    at_side(1, lambda p: from_side(1, p).wait_send())

    def settle_chunk(c):
        value_copy(last, c).wait_send()
        output_copy(last, c).wait_send()
        value_store(c).wait()
        output_store(c).wait()

    each(settle_chunk)
    for t in range(steps):
        mass_copy(t).wait_send()


def run_window(first, inputs, cotangent, value_weight, output_weight, mass, bias):
    groups = lax.axis_size("group")
    peers = lax.axis_size("fsdp")
    _, steps, positions, width = inputs.shape
    rows, inner = value_weight.shape[1:]
    own_inner = output_weight.shape[1]
    heads = bias.shape[0] // peers
    head_size = own_inner // heads
    batch = positions * peers
    o_cols = width // peers
    lanes = mass.shape[1]
    dma = pltpu.SemaphoreType.DMA
    hbm = pl.BlockSpec(memory_space=pl.ANY)
    vmem = pl.BlockSpec(memory_space=pltpu.VMEM)

    def chunk_of(step):
        return (rows, own_inner) if step % steps >= 2 else (own_inner, o_cols)

    relay_shape = (max(max(DETOUR[first]), 1), *chunk_of(3 - first))
    sizes = (groups, peers, steps, positions, heads, head_size)
    return pl.pallas_call(
        functools.partial(window_kernel, first, sizes),
        out_shape=(
            jax.ShapeDtypeStruct(value_weight.shape, BF16),
            jax.ShapeDtypeStruct(output_weight.shape, BF16),
            jax.ShapeDtypeStruct(mass.shape, F32),
        ),
        in_specs=[hbm, hbm, hbm, hbm, vmem, vmem],
        out_specs=(hbm, hbm, vmem),
        scratch_shapes=[
            pltpu.VMEM((steps, peers, positions, rows), BF16),
            pltpu.VMEM((rows, batch), BF16),
            pltpu.VMEM((steps, peers, positions, width), BF16),
            pltpu.VMEM((peers, rows, own_inner), F32),
            pltpu.VMEM((peers, own_inner, o_cols), F32),
            pltpu.VMEM((2, peers, rows, own_inner), BF16),
            pltpu.VMEM((2, peers, own_inner, o_cols), BF16),
            pltpu.VMEM((steps, *mass.shape), BF16),
            pltpu.VMEM((steps, peers, rows, own_inner), BF16),
            pltpu.VMEM((steps, peers, own_inner, o_cols), BF16),
            pltpu.VMEM((steps, *mass.shape), BF16),
            pltpu.VMEM((peers // 2, 2, batch, own_inner), BF16),
            pltpu.VMEM((steps, peers // 2, 2, batch, own_inner), BF16),
            pltpu.VMEM((batch, own_inner), BF16),
            pltpu.VMEM((steps, batch, own_inner), BF16),
            pltpu.VMEM(relay_shape, BF16),
            pltpu.VMEM((SIDE, *chunk_of(-first)), BF16),
            pltpu.VMEM((SIDE, *chunk_of(1 - first)), BF16),
            pltpu.VMEM((steps, peers, batch, own_inner), BF16),
            pltpu.VMEM((heads, batch, batch), BF16),
            pltpu.VMEM((heads, batch, batch), BF16),
            pltpu.VMEM((own_inner, batch), BF16),
            pltpu.VMEM((batch, own_inner), F32),
            pltpu.VMEM(mass.shape, F32),
            dma((2, peers)),
            dma((2,)),
            dma((2, peers)),
            dma((2, peers)),
            dma((steps, peers)),
            dma((steps, peers)),
            dma((steps, peers)),
            dma((steps, peers)),
            dma((steps, peers)),
            dma((steps, peers)),
            dma((steps, peers)),
            dma((steps, peers)),
            dma((steps, peers)),
            dma((steps, peers)),
            dma((steps,)),
            dma((steps,)),
            dma((steps,)),
            dma((steps,)),
            dma((peers,)),
            dma((peers,)),
            dma((2, peers)),
            dma((2, peers)),
        ],
        compiler_params=pltpu.CompilerParams(
            collective_id=first, has_side_effects=True, vmem_limit_bytes=63 << 20
        ),
        name="window",
    )(inputs, cotangent, value_weight, output_weight, mass, bias)


def on_device(
    inputs, cotangent, value_weight, output_weight, push_weight, position_bias, step_index
):
    mass = jnp.broadcast_to(push_weight[:, None], (16, 512))
    value_out, output_out, mass = lax.switch(
        step_index[0] % 4,
        [functools.partial(run_window, first) for first in range(4)],
        inputs,
        cotangent,
        value_weight,
        output_weight,
        mass,
        position_bias,
    )
    return (value_out, output_out, mass[0, :1])


def solution(mesh):
    placed = (
        P("group", None, "fsdp", None),
        P("group", None, "fsdp", None),
        P("group", "fsdp", None),
        P("group", "fsdp", None),
        P("group"),
        P(),
        P(),
    )
    return jax.shard_map(
        on_device,
        mesh=mesh,
        in_specs=placed,
        out_specs=(P("group", "fsdp", None), P("group", "fsdp", None), P("group")),
        check_vma=False,
    )
```
